128 devices in a mesh: dev: 128 (over y, x, z, core).
Axes of the slice: x: 4, y: 4, z: 4, core: 2. Of those that a mesh axis runs over, the one named last changes fastest.
Arguments:
- queries: bfloat16 [256, 32, 128], P('dev'), may hold values from -0.119628906 to 0.119628906
- passages: bfloat16 [65536, 64, 128], P('dev'), may hold values from -1.796875 to 1.796875
- lengths: int32 [65536], P('dev'), may hold values from 16 to 64
- candidates: int32 [256, 64], P('dev'), may hold values from 0 to 65535, as said below
Outputs:
- scores: float32 [256, 64], P('dev')
The draws below stay inside these ranges and needn't reach their ends.
Inputs may be any that keep to these rules, and one draw needn't show every extreme that they name: `candidates`: the 128 entries of the rows held by one device name, with repetition, at most 2 passages held by any one device (passage p is held by device p // 512), and exactly 2 for four devices; the passages of low number within each device are named far more often than the others, and a few devices are named far more often than the others over all rows.
All inputs are finite; a program needn't handle non-finite values.
Results may differ from the reference program's by a relative error of at most 0.0003.
Values may be sent and summed in bfloat16 or wider, within the bound.
A program may use at most 64 MiB of HBM per device.

```python
import jax
import jax.numpy as jnp
from jax import lax

DIM = 128
QTOK = 32
PTOK = 64
CAND = 64
Q_DEV = 2
P_DEV = 512
QUERIES = 256
NPASS = 65536
CAP = 2
N_DEV = 128


def draw_candidates(key, part):
    slots = Q_DEV * CAND
    count = N_DEV
    pool = jax.random.permutation(jax.random.fold_in(key, 1), count)[:8]

    def one_device(dkey):
        k_hot, k_rank, k_order, k_local = jax.random.split(dkey, 4)
        hot = pool[jax.random.permutation(k_hot, 8)[:4]]
        frequent_flag = jnp.zeros((count,), jnp.int32).at[hot].set(1)
        ranks = jax.random.permutation(k_rank, count).astype(jnp.int32)
        order = jnp.argsort(frequent_flag * count + ranks, stable=True)
        cold = order[:count - 4]
        index = jnp.arange(slots)
        hot_part = index < 4 * CAP
        owner = jnp.where(hot_part, hot[jnp.minimum(index // CAP, 3)], cold[(index - 4 * CAP) % (count - 4)])
        owner = owner[jax.random.permutation(k_order, slots)]
        draws = jax.random.randint(k_local, (slots,), 0, 1024)
        local = draws * draws // 1024 * draws // 1024 * P_DEV // 1024
        return (owner * P_DEV + local).astype(jnp.int32)
    keys = jax.random.split(jax.random.fold_in(key, 2), count)
    return jax.vmap(one_device)(keys).reshape(QUERIES, CAND)


def with_ends(values, key, smallest, largest):
    index_at = [jax.random.randint(jax.random.fold_in(key, axis), (), 0, length) for axis, length in enumerate(values.shape)]
    main_axis = values.shape.index(max(values.shape))
    beside = index_at[:main_axis] + [(index_at[main_axis] + 1) % values.shape[main_axis]] + index_at[main_axis + 1:]
    return values.at[tuple(index_at)].set(smallest).at[tuple(beside)].set(largest)


def level_of(rng, extent, shards, smallest, top_value):
    factor_of = 1.0
    for axis_at, shards_of in shards:
        steps = jax.random.uniform(jax.random.fold_in(jax.random.fold_in(rng, 6), axis_at), (shards_of,), jnp.float32, smallest / len(shards), top_value / len(shards))
        factor_of = factor_of * jnp.repeat(jnp.exp(steps), extent[axis_at] // shards_of).reshape((-1,) + (1,) * (len(extent) - 1 - axis_at))
    return factor_of


def scatter_about(rng, extent, spread, bound, pieces=(), kind=jnp.bfloat16):
    loudness = level_of(rng, extent, pieces, -0.22, 0.18) if pieces else 1.0
    array = jax.random.normal(rng, extent, jnp.float32) * spread * loudness
    return jnp.minimum(jnp.maximum(array, -bound), bound).astype(kind)


def setup_inputs(seed: int = 0) -> dict:
    splits = jax.random.split(jax.random.key(seed), 5)
    return {
        "queries": scatter_about(splits[0], (QUERIES, QTOK, DIM), 0.02, 0.119628906, ((0, 128),)),
        "passages": scatter_about(splits[1], (NPASS, PTOK, DIM), 0.3, 1.796875, ((0, 128),)),
        "lengths": with_ends(jax.random.randint(splits[2], (NPASS,), max(1, PTOK // 4), PTOK + 1), jax.random.fold_in(splits[2], 1), max(1, PTOK // 4), PTOK).astype(jnp.int32),
        "candidates": draw_candidates(jax.random.fold_in(splits[4], 71), 0),
    }


def reference(queries, passages, lengths, candidates):
    def one_query(item):
        query, ids = item
        block_groups = passages[ids].astype(jnp.float32)
        live = lengths[ids]
        similarity_matrix = jnp.einsum("qd,ctd->cqt", query.astype(jnp.float32), block_groups)
        keep = jnp.arange(PTOK)[None, None, :] < live[:, None, None]
        masked = jnp.where(keep, similarity_matrix, -1e30)
        return jnp.sum(jnp.max(masked, axis=2), axis=1)

    return lax.map(one_query, (queries, candidates))
```

```python
import functools

import jax
import jax.numpy as jnp
from jax import lax
from jax.experimental import pallas as pl
from jax.experimental.pallas import tpu as pltpu
from jax.sharding import PartitionSpec as P

MESH = pl.DeviceIdType.MESH
N_DEV = 128
STRIDE = {"z": 2, "x": 8, "y": 32}
PARTS = ((0, 32, "zyx"), (32, 16, "xzy"), (48, 16, "yxz"))


def shifted(me, axis, k):
    stride = STRIDE[axis]
    digit = (me // stride) % 4
    return me + stride * ((digit + k) % 4 - digit)


def place(order, dev):
    at = dev % 2
    for axis in reversed(order):
        at = at * 4 + (dev // STRIDE[axis]) % 4
    return at


def kernel(
    q_ref, pas_hbm, len_ref, cand_ref, out_ref,
    ga, gb, gc, codes, pas, codes_s, best, send, recv,
    q_send, q_recv, sib_send, sib_recv, c_send, c_recv, pas_sem, smem_sem, r_send, r_recv,
):
    me = lax.axis_index("dev")
    core = me % 2
    sibling = me + 1 - 2 * core
    bufs = (ga, gb, gc)

    pas_copy = pltpu.make_async_copy(pas_hbm, pas, pas_sem)
    pas_copy.start()

    barrier = pltpu.get_barrier_semaphore()
    near = [sibling]
    for axis in "zxy":
        for k in (1, 2, 3):
            near.append(shifted(me, axis, k))
    for k in (1, 2, 3):
        near.append(shifted(sibling, "z", k))
    for d in near:
        pl.semaphore_signal(barrier, inc=1, device_id=(d,), device_id_type=MESH)

    cand = cand_ref[...]
    row = jnp.concatenate([cand[0:1, :], cand[1:2, :]], axis=1)
    own_row = jnp.broadcast_to(row, (N_DEV, N_DEV))
    own_col = own_row.T
    sub = lax.broadcasted_iota(jnp.int32, (N_DEV, N_DEV), 0)
    lane = lax.broadcasted_iota(jnp.int32, (N_DEV, N_DEV), 1)
    asked = (own_col >> 9) == lane
    code = sub * 512 + (own_col & 511)
    first = jnp.min(jnp.where(asked, code, 1 << 20), axis=0, keepdims=True)
    last = jnp.max(jnp.where(asked, code, 0), axis=0, keepdims=True)
    packed = (first & 511) | ((last & 511) << 9)
    codes[me] = packed
    earlier = ((own_col >> 9) == (own_row >> 9)) & (sub < lane)
    rank = jnp.max(earlier.astype(jnp.int32), axis=0, keepdims=True)
    here = (own_row >> 9) == sub

    for (start, rows, order), g in zip(PARTS, bufs):
        g[place(order, me)] = q_ref[start // 32, start % 32 : start % 32 + rows, :]

    pl.semaphore_wait(barrier, len(near))

    def remote(src, dst, s, r, d):
        return pltpu.make_async_remote_copy(
            src_ref=src, dst_ref=dst, send_sem=s, recv_sem=r, device_id=(d,), device_id_type=MESH
        )

    sent = []

    def go(src, dst, s, r, d):
        c = remote(src, dst, s, r, d)
        c.start()
        sent.append(c)

    for i, d in enumerate([shifted(me, "z", k) for k in (1, 2, 3)] + [sibling] + [shifted(sibling, "z", k) for k in (1, 2, 3)]):
        go(codes.at[me], codes.at[me], c_send.at[i], c_recv.at[i], d)
    for p, ((_, rows, order), g) in enumerate(zip(PARTS, bufs)):
        at = place(order, me)
        for k in (1, 2, 3):
            go(g.at[at], g.at[at], q_send.at[p, 0, k - 1], q_recv.at[p, 0, k - 1], shifted(me, order[0], k))

    def arrived(ref, sem):
        pltpu.make_async_copy(ref, ref, sem).wait()

    base8 = (me // 8) * 8
    base32 = (me // 32) * 32
    for i in range(7):
        arrived(codes.at[0], c_recv.at[i])
    for k in (1, 2, 3):
        go(codes.at[pl.ds(base8, 8)], codes.at[pl.ds(base8, 8)], c_send.at[6 + k], c_recv.at[6 + k], shifted(me, "x", k))
    for phase in (1, 2):
        width = 4**phase
        for p, ((_, rows, order), g) in enumerate(zip(PARTS, bufs)):
            at = place(order, me) // width * width
            for k in (1, 2, 3):
                arrived(g.at[pl.ds(0, width // 4)], q_recv.at[p, phase - 1, k - 1])
            block = g.at[pl.ds(at, width)]
            for k in (1, 2, 3):
                go(block, block, q_send.at[p, phase, k - 1], q_recv.at[p, phase, k - 1], shifted(me, order[phase], k))
            if phase == 2:
                go(block, block, sib_send.at[p, 0], sib_recv.at[p, 0], sibling)
        if phase == 1:
            for k in (1, 2, 3):
                arrived(codes.at[pl.ds(0, 8)], c_recv.at[6 + k])
            for k in (1, 2, 3):
                go(codes.at[pl.ds(base32, 32)], codes.at[pl.ds(base32, 32)], c_send.at[9 + k], c_recv.at[9 + k], shifted(me, "y", k))
    for k in (1, 2, 3):
        arrived(codes.at[pl.ds(0, 32)], c_recv.at[9 + k])
    smem_copy = pltpu.make_async_copy(codes, codes_s, smem_sem)
    smem_copy.start()
    for k in (1, 2, 3):
        for p, ((_, rows, order), g) in enumerate(zip(PARTS, bufs)):
            arrived(g.at[pl.ds(0, 16)], q_recv.at[p, 2, k - 1])
            at = place(order, shifted(me, order[2], 4 - k)) // 16 * 16
            block = g.at[pl.ds(at, 16)]
            go(block, block, sib_send.at[p, k], sib_recv.at[p, k], sibling)
    pas_copy.wait()
    smem_copy.wait()
    for p, g in enumerate(bufs):
        for k in range(4):
            arrived(g.at[pl.ds(0, 16)], sib_recv.at[p, k])

    token = lax.broadcasted_iota(jnp.int32, (64, N_DEV), 0)
    half = lax.broadcasted_iota(jnp.int32, (1, N_DEV), 1) < 64

    def pair(j, carry):
        left = []
        lens = []
        right = []
        for r in (2 * j, 2 * j + 1):
            right += [g[place(order, r)] for (_, _, order), g in zip(PARTS, bufs)]
            both = codes_s[r, 0, me]
            for local in (both & 511, both >> 9):
                left.append(pas[local])
                lens.append(len_ref[local])
        sim = lax.dot_general(
            jnp.concatenate(left, axis=0), jnp.concatenate(right, axis=0),
            (((1,), (1,)), ((), ())), preferred_element_type=jnp.float32,
        )
        tops = []
        for i in range(4):
            s = jnp.where(token < lens[i], sim[64 * i : 64 * i + 64, :], -1e30)
            tops.append(jnp.max(s, axis=0, keepdims=True))
        best[0, j] = jnp.where(half, tops[0], tops[2])
        best[1, j] = jnp.where(half, tops[1], tops[3])
        return carry

    lane8 = lax.broadcasted_iota(jnp.int32, (8, N_DEV), 1)

    def group(i, carry):
        lax.fori_loop(8 * i, 8 * i + 8, pair, 0, unroll=True)
        sums = []
        for k in (0, 1):
            v = best[k, pl.ds(8 * i, 8), 0, :]
            for step in (1, 2, 4, 8, 16):
                up = pltpu.roll(v, N_DEV - step, 1)
                down = pltpu.roll(v, step, 1)
                v = v + jnp.where((lane8 // step) % 2 == 0, up, down)
            sums.append(v)
        low = lane8 < 64
        send[0, pl.ds(8 * i, 8), 0, :] = jnp.where(low, sums[0], pltpu.roll(sums[1], 64, 1))
        send[1, pl.ds(8 * i, 8), 0, :] = jnp.where(low, pltpu.roll(sums[0], 64, 1), sums[1])
        for t in range(16):
            r = 16 * i + t

            @pl.when(r != me)
            def _():
                remote(send.at[t % 2, 8 * i + t // 2], recv.at[me], r_send, r_recv, r).start()

            @pl.when(r == me)
            def _():
                recv[me] = send[t % 2, 8 * i + t // 2]

        return carry

    lax.fori_loop(0, 8, group, 0)
    done = remote(recv.at[pl.ds(0, N_DEV - 1)], recv.at[pl.ds(0, N_DEV - 1)], r_send, r_recv, sibling)
    done.wait_recv()

    got = recv[:, 0, :]
    by32, by64, by96 = (pltpu.roll(got, s, 1) for s in (32, 64, 96))
    k0 = jnp.where(lane < 32, got, jnp.where(lane < 96, by32, by64))
    k1 = jnp.where(lane < 32, by64, jnp.where(lane < 96, by96, got))
    mine = jnp.where(here, jnp.where(rank == 0, k0, k1), 0.0)
    total = jnp.sum(mine, axis=0, keepdims=True)
    out_ref[0:1, :] = total[:, :64]
    out_ref[1:2, :] = total[:, 64:]
    done.wait_send()
    for c in sent:
        c.wait_send()


def on_device(queries, passages, lengths, candidates):
    vmem = pl.BlockSpec(memory_space=pltpu.VMEM)
    dma = pltpu.SemaphoreType.DMA
    return pl.pallas_call(
        kernel,
        out_shape=jax.ShapeDtypeStruct((2, 64), jnp.float32),
        in_specs=[vmem, pl.BlockSpec(memory_space=pl.ANY), pl.BlockSpec(memory_space=pltpu.SMEM), vmem],
        out_specs=vmem,
        scratch_shapes=[
            *[pltpu.VMEM((N_DEV, rows, 128), jnp.bfloat16) for _, rows, _ in PARTS],
            pltpu.VMEM((N_DEV, 1, N_DEV), jnp.int32),
            pltpu.VMEM((512, 64, 128), jnp.bfloat16),
            pltpu.SMEM((N_DEV, 1, N_DEV), jnp.int32),
            pltpu.VMEM((2, 64, 1, N_DEV), jnp.float32),
            pltpu.VMEM((2, 64, 1, N_DEV), jnp.float32),
            pltpu.VMEM((N_DEV, 1, N_DEV), jnp.float32),
            dma((3, 3, 3)), dma((3, 3, 3)),
            dma((3, 4)), dma((3, 4)),
            dma((13,)), dma((13,)),
            dma, dma, dma, dma,
        ],
        compiler_params=pltpu.CompilerParams(
            collective_id=0, has_side_effects=True, vmem_limit_bytes=48 * 1024 * 1024
        ),
    )(queries, passages, lengths, candidates)


def solution(mesh):
    return jax.shard_map(
        on_device,
        mesh=mesh,
        in_specs=(P("dev", None, None), P("dev", None, None), P("dev"), P("dev", None)),
        out_specs=P("dev", None),
        check_vma=False,
    )
```
